32 devices in a mesh: seq: 8 (over z, x), rep: 4 (over y, core).
Axes of the slice: x: 2, y: 2, z: 4, core: 2. Of those that a mesh axis runs over, the one named last changes fastest.
Arguments:
- queries: bfloat16 [4096, 8192], P(('rep', 'seq')), may hold values from -6 to 6
- keys: bfloat16 [4096, 1024], P(('rep', 'seq')), may hold values from -6 to 6
- values: bfloat16 [4096, 1024], P(('rep', 'seq')), may hold values from -6 to 6
- vertical: int32 [64, 24], replicated, may hold values from -1 to 63, as said below
- slash: int32 [64, 24], replicated, may hold values from -1 to 63, as said below
Outputs:
- attention: bfloat16 [4096, 8192], P(('rep', 'seq'))
The draws below stay inside these ranges and needn't reach their ends.
Inputs may be any that keep to these rules, and one draw needn't show every extreme that they name: `vertical`: in each row the entries other than -1 come first and are distinct; every row has at least one; some row has all 24 in use. `slash`: each row begins with 0; the entries other than -1 come first and are distinct; some row has all 24 in use.
All inputs are finite; a program needn't handle non-finite values.
Results may differ from the reference program's by a relative error of at most 0.0055.
Values may be sent and summed in bfloat16 or wider, within the bound.
A program may use at most 128 MiB of HBM per device.

```python
import math
import jax
import jax.numpy as jnp
from jax import lax

QUERY_HEADS = 64
KEY_VALUE_HEADS = 8
HEAD_SIZE = 128
BLOCK = 64
NV = 24
NS = 24
PROMPT_TOKENS = 4096


def mask_table(key, slot_count, leading_zero):
    block_count = PROMPT_TOKENS // BLOCK
    head_keys = jax.random.split(jax.random.fold_in(key, 3), QUERY_HEADS)

    def permuted_row(row_key):
        if leading_zero:
            return jax.random.permutation(row_key, block_count - 1)[:slot_count - 1].astype(jnp.int32) + 1
        return jax.random.permutation(row_key, block_count)[:slot_count].astype(jnp.int32)
    table = jax.vmap(permuted_row)(head_keys)
    if leading_zero:
        table = jnp.concatenate([jnp.zeros((QUERY_HEADS, 1), jnp.int32), table], axis=1)
    fixed_slot = 1 if leading_zero else 0
    heavy = jax.random.randint(jax.random.fold_in(key, 4), (), 0, QUERY_HEADS, dtype=jnp.int32)
    light = (heavy + 1) % QUERY_HEADS
    row_index = jnp.arange(QUERY_HEADS, dtype=jnp.int32)[:, None]
    slot_index = jnp.arange(slot_count, dtype=jnp.int32)[None, :]
    heavy_row = row_index == heavy
    last_block = block_count - 1
    held = table[heavy, fixed_slot]
    table = jnp.where(heavy_row & (table == last_block), held, table)
    table = jnp.where(heavy_row & (slot_index == fixed_slot), last_block, table)
    counts = jax.random.randint(jax.random.fold_in(key, 5), (QUERY_HEADS,), 1, slot_count + 1, dtype=jnp.int32)
    counts = jnp.where(row_index[:, 0] == heavy, slot_count, counts)
    counts = jnp.where(row_index[:, 0] == light, 1, counts)
    return jnp.where(slot_index < counts[:, None], table, -1).astype(jnp.int32)


def draw_vertical(key, part):
    return mask_table(jax.random.fold_in(key, 101), NV, False)


def draw_slash(key, part):
    return mask_table(jax.random.fold_in(key, 202), NS, True)


def draw_queries(key, part):
    sampled_rows = jnp.clip(jax.random.normal(jax.random.fold_in(key, 1), (PROMPT_TOKENS, QUERY_HEADS, HEAD_SIZE), jnp.float32), -6.0, 6.0)
    return sampled_rows.reshape(PROMPT_TOKENS, QUERY_HEADS * HEAD_SIZE).astype(jnp.bfloat16)


def draw_keys(key, part):
    sampled_rows = jnp.clip(jax.random.normal(jax.random.fold_in(key, 2), (PROMPT_TOKENS, KEY_VALUE_HEADS, HEAD_SIZE), jnp.float32), -6.0, 6.0)
    return sampled_rows.reshape(PROMPT_TOKENS, KEY_VALUE_HEADS * HEAD_SIZE).astype(jnp.bfloat16)


def block_levels(key, extent, pieces, smallest, high):
    loudness = 1.0
    for dim, blocks in pieces:
        heights = jax.random.uniform(jax.random.fold_in(jax.random.fold_in(key, 6), dim), (blocks,), jnp.float32, smallest / len(pieces), high / len(pieces))
        loudness = loudness * jnp.repeat(jnp.exp(heights), extent[dim] // blocks).reshape((-1,) + (1,) * (len(extent) - 1 - dim))
    return loudness


def normal_values(key, extent, deviation, reach, cuts=(), kind=jnp.bfloat16):
    drawn = deviation * jax.random.normal(key, extent, jnp.float32)
    if cuts:
        drawn = drawn * block_levels(key, extent, cuts, -0.22, 0.18)
    return jnp.clip(drawn, -reach, reach).astype(kind)


def setup_inputs(seed: int = 0) -> dict:
    seeds = jax.random.split(jax.random.key(seed), 6)
    queries = draw_queries(jax.random.fold_in(seeds[5], 71), 0)
    keys = draw_keys(jax.random.fold_in(seeds[5], 71), 0)
    values = normal_values(seeds[2], (PROMPT_TOKENS, KEY_VALUE_HEADS * HEAD_SIZE), 1.0, 6.0, ((0, 32),))
    vertical = draw_vertical(jax.random.fold_in(seeds[5], 71), 0)
    slash = draw_slash(jax.random.fold_in(seeds[5], 71), 0)
    return dict(queries=queries, keys=keys, values=values, vertical=vertical, slash=slash)


def head_attention(query_rows, key_rows, value_rows, columns, offsets):
    block_count = PROMPT_TOKENS // BLOCK
    logit_scale = 1.0 / math.sqrt(HEAD_SIZE)
    query_block_list = query_rows.reshape(block_count, BLOCK, HEAD_SIZE)
    key_blocks = key_rows.reshape(block_count, BLOCK, HEAD_SIZE)
    value_blocks = value_rows.reshape(block_count, BLOCK, HEAD_SIZE)
    blocks = jnp.arange(block_count, dtype=jnp.int32)
    within = jnp.arange(BLOCK, dtype=jnp.int32)
    causal = within[None, :] <= within[:, None]
    column_ok = (columns >= 0)[None, :] & (columns[None, :] <= blocks[:, None])
    sources = blocks[:, None] - offsets[None, :]
    repeated = jnp.any(sources[:, :, None] == columns[None, None, :], axis=2)
    offset_ok = (offsets >= 0)[None, :] & (sources >= 0) & jnp.logical_not(repeated)
    picked = jnp.concatenate([jnp.broadcast_to(columns[None, :], (block_count, columns.shape[0])), sources], axis=1).astype(jnp.int32)
    picked_ok = jnp.concatenate([column_ok, offset_ok], axis=1)
    safe_pick = jnp.clip(picked, 0, block_count - 1).astype(jnp.int32)
    group_size = math.gcd(block_count, 64)

    def one_group(group_start):
        current_rows = lax.dynamic_slice_in_dim(query_block_list, group_start, group_size, 0).astype(jnp.float32)
        picks_here = lax.dynamic_slice_in_dim(safe_pick, group_start, group_size, 0)
        raw_here = lax.dynamic_slice_in_dim(picked, group_start, group_size, 0)
        ok_here = lax.dynamic_slice_in_dim(picked_ok, group_start, group_size, 0)
        blocks_here = lax.dynamic_slice_in_dim(blocks, group_start, group_size, 0)
        key_selected = key_blocks[picks_here].astype(jnp.float32)
        value_selected = value_blocks[picks_here].astype(jnp.float32)
        attention_logits = jnp.einsum('zja,zmga->zjmg', current_rows, key_selected) * logit_scale
        earlier = (raw_here < blocks_here[:, None])[:, None, :, None]
        token_ok = ok_here[:, None, :, None] & (earlier | causal[None, :, None, :])
        masked = jnp.where(token_ok, attention_logits, -jnp.inf)
        row_top = lax.optimization_barrier(jnp.max(masked, axis=(2, 3), keepdims=True))
        softmax_weights = jnp.where(token_ok, jnp.exp(masked - row_top), 0.0)
        totals = lax.optimization_barrier(jnp.sum(softmax_weights, axis=(2, 3)))
        rounded_length = lax.optimization_barrier(softmax_weights.astype(jnp.bfloat16)).astype(jnp.float32)
        blended_values = jnp.einsum('xgmj,xmjf->xgf', rounded_length, value_selected)
        return (blended_values / totals[..., None]).astype(jnp.bfloat16)
    group_starts = jnp.arange(0, block_count, group_size, dtype=jnp.int32)
    results = lax.map(one_group, group_starts)
    return results.reshape(PROMPT_TOKENS, HEAD_SIZE)

def reference(queries, keys, values, vertical, slash):
    query_heads = queries.reshape(PROMPT_TOKENS, QUERY_HEADS, HEAD_SIZE)
    key_head_group = keys.reshape(PROMPT_TOKENS, KEY_VALUE_HEADS, HEAD_SIZE)
    value_head_group = values.reshape(PROMPT_TOKENS, KEY_VALUE_HEADS, HEAD_SIZE)
    heads_per_group = QUERY_HEADS // KEY_VALUE_HEADS

    def one_head(head_index):
        key_head = head_index // heads_per_group
        return head_attention(query_heads[:, head_index], key_head_group[:, key_head], value_head_group[:, key_head], vertical[head_index], slash[head_index])
    results = lax.map(one_head, jnp.arange(QUERY_HEADS, dtype=jnp.int32))
    return jnp.transpose(results, (1, 0, 2)).reshape(PROMPT_TOKENS, QUERY_HEADS * HEAD_SIZE)
```

```python
import functools
import math

import jax
import jax.numpy as jnp
from jax import lax
from jax.experimental import pallas as pl
from jax.experimental.pallas import tpu as pltpu
from jax.sharding import PartitionSpec as P

QUERY_HEADS = 64
KEY_VALUE_HEADS = 8
HEAD_SIZE = 128
BLOCK = 64
GROUP = QUERY_HEADS // KEY_VALUE_HEADS

MASKED = -1e30
KEY_TILE = 1024
ROW_TILE = 256
EXP2_SCALE = math.log2(math.e) / math.sqrt(HEAD_SIZE)


def attend_kernel(first_head, rows, position_ref, q_ref, k_ref, v_ref, mask_ref, own_mask_ref, *rest):
    out_ref, query_s, best_s, acc_s = rest[-4:]
    blocks = rows // BLOCK
    position = position_ref[0]
    head_base = (first_head + pl.program_id(0)) * GROUP
    lane = lax.broadcasted_iota(jnp.int32, (rows, HEAD_SIZE), 1)
    row_block = lax.broadcasted_iota(jnp.int32, (rows, HEAD_SIZE), 0) // BLOCK
    for head in range(GROUP):
        pick = lane == (head_base + head) * blocks + row_block
        query_s[head * rows : (head + 1) * rows, :HEAD_SIZE] = q_ref[
            :, head * HEAD_SIZE : (head + 1) * HEAD_SIZE
        ]
        query_s[head * rows : (head + 1) * rows, HEAD_SIZE:] = pick.astype(jnp.bfloat16)

    row_tile = min(ROW_TILE, GROUP * rows)
    tiles = [slice(i, i + row_tile) for i in range(0, GROUP * rows, row_tile)]
    contract = (((1,), (1,)), ((), ()))

    own = pl.ds(pl.multiple_of(position * rows, rows), rows)
    own_keys = jnp.concatenate([k_ref[own, :], own_mask_ref[...]], axis=1)
    own_values = jnp.concatenate([v_ref[own, :], jnp.ones((rows, HEAD_SIZE), jnp.bfloat16)], axis=1)
    own_row = lax.broadcasted_iota(jnp.int32, (row_tile, rows), 0) % rows
    own_column = lax.broadcasted_iota(jnp.int32, (row_tile, rows), 1)
    for tile in tiles:
        scores = lax.dot_general(
            query_s[tile, :], own_keys, contract, preferred_element_type=jnp.float32
        )
        scores = jnp.where(own_column <= own_row, scores, MASKED)
        best = jnp.max(scores, axis=1, keepdims=True)
        weights = jnp.exp2((scores - best) * EXP2_SCALE).astype(jnp.bfloat16)
        best_s[tile, :] = jnp.broadcast_to(best, (row_tile, HEAD_SIZE))
        acc_s[tile, :] = jnp.dot(weights, own_values, preferred_element_type=jnp.float32)

    def key_step(step, _):
        here = pl.ds(pl.multiple_of(step * KEY_TILE, KEY_TILE), KEY_TILE)
        keys = jnp.concatenate([k_ref[here, :], mask_ref[here, :]], axis=1)
        values = jnp.concatenate(
            [v_ref[here, :], jnp.ones((KEY_TILE, HEAD_SIZE), jnp.bfloat16)], axis=1
        )
        for tile in tiles:
            scores = lax.dot_general(
                query_s[tile, :], keys, contract, preferred_element_type=jnp.float32
            )
            before = best_s[tile, :1]
            best = jnp.maximum(before, jnp.max(scores, axis=1, keepdims=True))
            factor = jnp.exp2((before - best) * EXP2_SCALE)
            weights = jnp.exp2((scores - best) * EXP2_SCALE).astype(jnp.bfloat16)
            best_s[tile, :] = jnp.broadcast_to(best, (row_tile, HEAD_SIZE))
            acc_s[tile, :] = acc_s[tile, :] * factor + jnp.dot(
                weights, values, preferred_element_type=jnp.float32
            )
        return 0

    lax.fori_loop(0, (position * rows + KEY_TILE - 1) // KEY_TILE, key_step, 0)

    for head in range(GROUP):
        tile = slice(head * rows, (head + 1) * rows)
        out_ref[:, head * HEAD_SIZE : (head + 1) * HEAD_SIZE] = (
            acc_s[tile, :HEAD_SIZE] / acc_s[tile, HEAD_SIZE:]
        ).astype(jnp.bfloat16)


def attend(position, queries, gathered, mask, own_mask, out, first_head, heads):
    rows = queries.shape[0]
    tokens = gathered.shape[0]
    once = pl.Buffered(1)
    in_specs = [
        pl.BlockSpec((rows, GROUP * HEAD_SIZE), lambda g, s: (0, first_head + g)),
        pl.BlockSpec((tokens, HEAD_SIZE), lambda g, s: (0, g)),
        pl.BlockSpec((tokens, HEAD_SIZE), lambda g, s: (0, heads + g)),
        pl.BlockSpec((tokens, HEAD_SIZE), lambda g, s: (0, 0), pipeline_mode=once),
        pl.BlockSpec((rows, HEAD_SIZE), lambda g, s: (0, 0), pipeline_mode=once),
    ]
    operands = [position, queries, gathered, gathered, mask, own_mask]
    aliases = {}
    if out is not None:
        in_specs.append(pl.BlockSpec(memory_space=pl.ANY))
        aliases = {len(operands): 0}
        operands.append(out)
    pairs = heads * GROUP * rows * tokens
    return pl.pallas_call(
        functools.partial(attend_kernel, first_head, rows),
        out_shape=jax.ShapeDtypeStruct(queries.shape, jnp.bfloat16),
        grid_spec=pltpu.PrefetchScalarGridSpec(
            num_scalar_prefetch=1,
            grid=(heads,),
            in_specs=in_specs,
            out_specs=pl.BlockSpec((rows, GROUP * HEAD_SIZE), lambda g, s: (0, first_head + g)),
            scratch_shapes=[
                pltpu.VMEM((GROUP * rows, 2 * HEAD_SIZE), jnp.bfloat16),
                pltpu.VMEM((GROUP * rows, HEAD_SIZE), jnp.float32),
                pltpu.VMEM((GROUP * rows, 2 * HEAD_SIZE), jnp.float32),
            ],
        ),
        input_output_aliases=aliases,
        compiler_params=pltpu.CompilerParams(
            vmem_limit_bytes=60 << 20
        ),
        cost_estimate=pl.CostEstimate(
            flops=pairs * HEAD_SIZE * 8,
            bytes_accessed=heads * tokens * HEAD_SIZE * 4,
            transcendentals=pairs,
        ),
    )(*operands)


def mask_columns(vertical, slash, first_block, blocks, block_total):
    key_block = jnp.arange(block_total, dtype=jnp.int32)
    here = first_block + jnp.arange(blocks, dtype=jnp.int32)
    column = jnp.any(vertical[None] == key_block[:, None, None], axis=-1)
    gap = here[None, :] - key_block[:, None]
    diagonal = jnp.any(slash[None, :, None, :] == gap[:, None, :, None], axis=-1)
    allowed = column[:, :, None] | diagonal
    earlier = (key_block < first_block)[:, None, None]
    width = QUERY_HEADS * blocks

    def spread(keep):
        fill = jnp.where(keep, 0.0, MASKED).astype(jnp.bfloat16).reshape(-1, width)
        return jnp.repeat(fill, BLOCK, axis=0)

    own = lax.dynamic_slice_in_dim(allowed, first_block, blocks, 0)
    return spread(allowed & earlier), spread(own)


def body(queries, keys, values, vertical, slash):
    rows = queries.shape[0]
    ways = lax.axis_size("rep") * lax.axis_size("seq")
    tokens = rows * ways
    position = lax.axis_index("rep") * lax.axis_size("seq") + lax.axis_index("seq")
    total_bytes = 2 * tokens * keys.shape[1] * keys.dtype.itemsize
    tight = total_bytes > (32 << 20)
    heads = 1 if tight else 2
    mask, own_mask = mask_columns(
        vertical, slash, position * (rows // BLOCK), rows // BLOCK, tokens // BLOCK
    )
    position = position.astype(jnp.int32).reshape(1)
    out = None
    for first in range(0, KEY_VALUE_HEADS, heads):
        columns = slice(first * HEAD_SIZE, (first + heads) * HEAD_SIZE)
        part = jnp.concatenate([keys[:, columns], values[:, columns]], axis=1)
        if tight and out is not None:
            part, out = lax.optimization_barrier((part, out))
        gathered = lax.all_gather(part, ("rep", "seq"), axis=0, tiled=True)
        out = attend(position, queries, gathered, mask, own_mask, out, first, heads)
    return out


def solution(mesh):
    in_specs = (P(("rep", "seq"), None), P(("rep", "seq"), None), P(("rep", "seq"), None), P(), P())
    out_specs = P(("rep", "seq"), None)
    return jax.shard_map(body, mesh=mesh, in_specs=in_specs, out_specs=out_specs, check_vma=False)
```

```python
import functools
import math

import jax
import jax.numpy as jnp
from jax import lax
from jax.experimental import pallas as pl
from jax.experimental.pallas import tpu as pltpu
from jax.sharding import PartitionSpec as P

QUERY_HEADS = 64
KEY_VALUE_HEADS = 8
HEAD_SIZE = 128
BLOCK = 64
GROUP = QUERY_HEADS // KEY_VALUE_HEADS

MASKED = -1e30
KEY_TILE = 1024
ROW_TILE = 256
EXP2_SCALE = math.log2(math.e) / math.sqrt(HEAD_SIZE)


def attend_kernel(first_head, rows, position_ref, q_ref, k_ref, v_ref, mask_ref, own_mask_ref, *rest):
    out_ref, query_s, best_s, acc_s = rest[-4:]
    blocks = rows // BLOCK
    position = position_ref[0]
    head_base = (first_head + pl.program_id(0)) * GROUP
    lane = lax.broadcasted_iota(jnp.int32, (rows, HEAD_SIZE), 1)
    row_block = lax.broadcasted_iota(jnp.int32, (rows, HEAD_SIZE), 0) // BLOCK
    for head in range(GROUP):
        pick = lane == (head_base + head) * blocks + row_block
        query_s[head * rows : (head + 1) * rows, :HEAD_SIZE] = q_ref[
            :, head * HEAD_SIZE : (head + 1) * HEAD_SIZE
        ]
        query_s[head * rows : (head + 1) * rows, HEAD_SIZE:] = pick.astype(jnp.bfloat16)

    row_tile = min(ROW_TILE, GROUP * rows)
    tiles = [slice(i, i + row_tile) for i in range(0, GROUP * rows, row_tile)]
    contract = (((1,), (1,)), ((), ()))

    own = pl.ds(pl.multiple_of(position * rows, rows), rows)
    own_keys = jnp.concatenate([k_ref[own, :], own_mask_ref[...]], axis=1)
    own_values = jnp.concatenate([v_ref[own, :], jnp.ones((rows, HEAD_SIZE), jnp.bfloat16)], axis=1)
    own_row = lax.broadcasted_iota(jnp.int32, (row_tile, rows), 0) % rows
    own_column = lax.broadcasted_iota(jnp.int32, (row_tile, rows), 1)
    for tile in tiles:
        scores = lax.dot_general(
            query_s[tile, :], own_keys, contract, preferred_element_type=jnp.float32
        )
        scores = jnp.where(own_column <= own_row, scores, MASKED)
        best = jnp.max(scores, axis=1, keepdims=True)
        weights = jnp.exp2((scores - best) * EXP2_SCALE).astype(jnp.bfloat16)
        best_s[tile, :] = jnp.broadcast_to(best, (row_tile, HEAD_SIZE))
        acc_s[tile, :] = jnp.dot(weights, own_values, preferred_element_type=jnp.float32)

    def key_step(step, _):
        here = pl.ds(pl.multiple_of(step * KEY_TILE, KEY_TILE), KEY_TILE)
        keys = jnp.concatenate([k_ref[here, :], mask_ref[here, :]], axis=1)
        values = jnp.concatenate(
            [v_ref[here, :], jnp.ones((KEY_TILE, HEAD_SIZE), jnp.bfloat16)], axis=1
        )
        for tile in tiles:
            scores = lax.dot_general(
                query_s[tile, :], keys, contract, preferred_element_type=jnp.float32
            )
            before = best_s[tile, :1]
            best = jnp.maximum(before, jnp.max(scores, axis=1, keepdims=True))
            factor = jnp.exp2((before - best) * EXP2_SCALE)
            weights = jnp.exp2((scores - best) * EXP2_SCALE).astype(jnp.bfloat16)
            best_s[tile, :] = jnp.broadcast_to(best, (row_tile, HEAD_SIZE))
            acc_s[tile, :] = acc_s[tile, :] * factor + jnp.dot(
                weights, values, preferred_element_type=jnp.float32
            )
        return 0

    lax.fori_loop(0, (position * rows + KEY_TILE - 1) // KEY_TILE, key_step, 0)

    for head in range(GROUP):
        tile = slice(head * rows, (head + 1) * rows)
        out_ref[:, head * HEAD_SIZE : (head + 1) * HEAD_SIZE] = (
            acc_s[tile, :HEAD_SIZE] / acc_s[tile, HEAD_SIZE:]
        ).astype(jnp.bfloat16)


def attend(position, queries, gathered, mask, own_mask, out, first_head, heads):
    rows = queries.shape[0]
    tokens = gathered.shape[0]
    once = pl.Buffered(1)
    in_specs = [
        pl.BlockSpec((rows, GROUP * HEAD_SIZE), lambda g, s: (0, first_head + g)),
        pl.BlockSpec((tokens, HEAD_SIZE), lambda g, s: (0, g)),
        pl.BlockSpec((tokens, HEAD_SIZE), lambda g, s: (0, heads + g)),
        pl.BlockSpec((tokens, HEAD_SIZE), lambda g, s: (0, 0), pipeline_mode=once),
        pl.BlockSpec((rows, HEAD_SIZE), lambda g, s: (0, 0), pipeline_mode=once),
    ]
    operands = [position, queries, gathered, gathered, mask, own_mask]
    aliases = {}
    if out is not None:
        in_specs.append(pl.BlockSpec(memory_space=pl.ANY))
        aliases = {len(operands): 0}
        operands.append(out)
    pairs = heads * GROUP * rows * tokens
    return pl.pallas_call(
        functools.partial(attend_kernel, first_head, rows),
        out_shape=jax.ShapeDtypeStruct(queries.shape, jnp.bfloat16),
        grid_spec=pltpu.PrefetchScalarGridSpec(
            num_scalar_prefetch=1,
            grid=(heads,),
            in_specs=in_specs,
            out_specs=pl.BlockSpec((rows, GROUP * HEAD_SIZE), lambda g, s: (0, first_head + g)),
            scratch_shapes=[
                pltpu.VMEM((GROUP * rows, 2 * HEAD_SIZE), jnp.bfloat16),
                pltpu.VMEM((GROUP * rows, HEAD_SIZE), jnp.float32),
                pltpu.VMEM((GROUP * rows, 2 * HEAD_SIZE), jnp.float32),
            ],
        ),
        input_output_aliases=aliases,
        compiler_params=pltpu.CompilerParams(
            vmem_limit_bytes=60 << 20
        ),
        cost_estimate=pl.CostEstimate(
            flops=pairs * HEAD_SIZE * 8,
            bytes_accessed=heads * tokens * HEAD_SIZE * 4,
            transcendentals=pairs,
        ),
    )(*operands)


def fused_kernel(
    chunk, q_ref, key_ref, value_ref, mask_ref, own_mask_ref, out_ref,
    pool, query_s, best_s, acc_s, send_sem, recv_sem,
):
    rows = key_ref.shape[0]
    depth = pool.shape[4]
    blocks = rows // BLOCK
    seq, rep = lax.axis_index("seq"), lax.axis_index("rep")
    z, x, y, core = seq // 2, seq % 2, rep // 2, rep % 2
    z_peers = [((z + k) % depth) * 2 + x for k in range(1, depth)]
    along_x = {"seq": z * 2 + 1 - x, "rep": rep}
    along_y = {"seq": seq, "rep": (1 - y) * 2 + core}
    sibling = {"seq": seq, "rep": y * 2 + 1 - core}
    peers = [{"seq": peer, "rep": rep} for peer in z_peers] + [along_x, along_y, sibling]

    for head in range(KEY_VALUE_HEADS):
        columns = slice(head * HEAD_SIZE, (head + 1) * HEAD_SIZE)
        pool[0, head, y, core, z, x] = key_ref[:, columns]
        pool[1, head, y, core, z, x] = value_ref[:, columns]

    barrier = pltpu.get_barrier_semaphore()
    for peer in peers:
        pl.semaphore_signal(
            barrier, inc=1, device_id=peer, device_id_type=pl.DeviceIdType.MESH
        )
    pl.semaphore_wait(barrier, len(peers))

    copies = {}

    def send(kind, part, slot, ref, peer):
        copy = pltpu.make_async_remote_copy(
            src_ref=ref,
            dst_ref=ref,
            send_sem=send_sem.at[kind, part, slot],
            recv_sem=recv_sem.at[kind, part, slot],
            device_id=peer,
            device_id_type=pl.DeviceIdType.MESH,
        )
        copy.start()
        copies[kind, part, slot] = copy

    def heads_of(part):
        return pl.ds(part * chunk, chunk)

    def stage_line(part):
        for kind in range(2):
            for k in range(depth - 1):
                send(kind, part, k, pool.at[kind, heads_of(part), y, core, z, x], peers[k])

    def stage_first(part):
        for kind in range(2):
            for k in range(depth - 1):
                copies[kind, part, k].wait_recv()
            send(
                kind, part, depth - 1, pool.at[kind, heads_of(part), y, core, :, x],
                along_y if kind else along_x,
            )

    def stage_second(part):
        for kind in range(2):
            copies[kind, part, depth - 1].wait_recv()
        send(0, part, depth, pool.at[0, heads_of(part), y, core], along_y)
        send(1, part, depth, pool.at[1, heads_of(part), :, core, :, x], along_x)

    def stage_core(part):
        for kind in range(2):
            copies[kind, part, depth].wait_recv()
            send(kind, part, depth + 1, pool.at[kind, heads_of(part), :, core], sibling)

    def stage_done(part):
        for kind in range(2):
            copies[kind, part, depth + 1].wait_recv()

    key_tile = depth * 2 * rows
    steps = rep + (seq + 2 * depth - 1) // (2 * depth)
    row_tile = min(ROW_TILE, GROUP * rows)
    tiles = [slice(i, i + row_tile) for i in range(0, GROUP * rows, row_tile)]
    contract = (((1,), (1,)), ((), ()))

    def attend_group(group):
        lane = lax.broadcasted_iota(jnp.int32, (rows, HEAD_SIZE), 1)
        row_block = lax.broadcasted_iota(jnp.int32, (rows, HEAD_SIZE), 0) // BLOCK
        for local in range(GROUP):
            head = group * GROUP + local
            here = slice(local * rows, (local + 1) * rows)
            query_s[here, :HEAD_SIZE] = q_ref[:, head * HEAD_SIZE : (head + 1) * HEAD_SIZE]
            query_s[here, HEAD_SIZE:] = (lane == head * blocks + row_block).astype(jnp.bfloat16)

        own_keys = jnp.concatenate([pool[0, group, y, core, z, x], own_mask_ref[...]], axis=1)
        own_values = jnp.concatenate(
            [pool[1, group, y, core, z, x], jnp.ones((rows, HEAD_SIZE), jnp.bfloat16)], axis=1
        )
        own_row = lax.broadcasted_iota(jnp.int32, (row_tile, rows), 0) % rows
        own_column = lax.broadcasted_iota(jnp.int32, (row_tile, rows), 1)
        for tile in tiles:
            scores = lax.dot_general(
                query_s[tile, :], own_keys, contract, preferred_element_type=jnp.float32
            )
            scores = jnp.where(own_column <= own_row, scores, MASKED)
            best = jnp.max(scores, axis=1, keepdims=True)
            weights = jnp.exp2((scores - best) * EXP2_SCALE).astype(jnp.bfloat16)
            best_s[tile, :] = jnp.broadcast_to(best, (row_tile, HEAD_SIZE))
            acc_s[tile, :] = jnp.dot(weights, own_values, preferred_element_type=jnp.float32)

        def key_step(step, _):
            here = pl.ds(pl.multiple_of(step * key_tile, key_tile), key_tile)
            key_rows = pool[0, group, step // 2, step % 2].reshape(key_tile, HEAD_SIZE)
            value_rows = pool[1, group, step // 2, step % 2].reshape(key_tile, HEAD_SIZE)
            keys = jnp.concatenate([key_rows, mask_ref[here, :]], axis=1)
            values = jnp.concatenate(
                [value_rows, jnp.ones((key_tile, HEAD_SIZE), jnp.bfloat16)], axis=1
            )
            for tile in tiles:
                scores = lax.dot_general(
                    query_s[tile, :], keys, contract, preferred_element_type=jnp.float32
                )
                before = best_s[tile, :1]
                best = jnp.maximum(before, jnp.max(scores, axis=1, keepdims=True))
                factor = jnp.exp2((before - best) * EXP2_SCALE)
                weights = jnp.exp2((scores - best) * EXP2_SCALE).astype(jnp.bfloat16)
                best_s[tile, :] = jnp.broadcast_to(best, (row_tile, HEAD_SIZE))
                acc_s[tile, :] = acc_s[tile, :] * factor + jnp.dot(
                    weights, values, preferred_element_type=jnp.float32
                )
            return 0

        lax.fori_loop(0, steps, key_step, 0)
        for local in range(GROUP):
            head = group * GROUP + local
            tile = slice(local * rows, (local + 1) * rows)
            out_ref[:, head * HEAD_SIZE : (head + 1) * HEAD_SIZE] = (
                acc_s[tile, :HEAD_SIZE] / acc_s[tile, HEAD_SIZE:]
            ).astype(jnp.bfloat16)

    for part in range(4):
        stage_line(part)
    stage_first(0)
    stage_second(0)
    stage_first(1)
    stage_core(0)
    stage_done(0)
    attend_group(0)
    stage_first(2)
    stage_second(1)
    attend_group(1)
    stage_first(3)
    stage_core(1)
    stage_second(2)
    stage_done(1)
    attend_group(2)
    stage_second(3)
    stage_core(2)
    attend_group(3)
    stage_core(3)
    stage_done(2)
    attend_group(4)
    attend_group(5)
    stage_done(3)
    attend_group(6)
    attend_group(7)
    for copy in copies.values():
        copy.wait_send()


def fused(queries, keys, values, mask, own_mask, depth):
    rows = queries.shape[0]
    parts = 4
    tokens = mask.shape[0]
    pairs = QUERY_HEADS * rows * tokens
    whole = pl.BlockSpec(memory_space=pltpu.VMEM)
    return pl.pallas_call(
        functools.partial(fused_kernel, KEY_VALUE_HEADS // parts),
        out_shape=jax.ShapeDtypeStruct(queries.shape, jnp.bfloat16),
        in_specs=[whole] * 5,
        out_specs=whole,
        scratch_shapes=[
            pltpu.VMEM((2, KEY_VALUE_HEADS, 2, 2, depth, 2, rows, HEAD_SIZE), jnp.bfloat16),
            pltpu.VMEM((GROUP * rows, 2 * HEAD_SIZE), jnp.bfloat16),
            pltpu.VMEM((GROUP * rows, HEAD_SIZE), jnp.float32),
            pltpu.VMEM((GROUP * rows, 2 * HEAD_SIZE), jnp.float32),
            pltpu.SemaphoreType.DMA((2, parts, depth + 2)),
            pltpu.SemaphoreType.DMA((2, parts, depth + 2)),
        ],
        compiler_params=pltpu.CompilerParams(
            collective_id=0, has_side_effects=True, vmem_limit_bytes=56 << 20
        ),
        cost_estimate=pl.CostEstimate(
            flops=pairs * HEAD_SIZE * 8, bytes_accessed=8 << 20, transcendentals=pairs
        ),
    )(queries, keys, values, mask, own_mask)


def mask_columns(vertical, slash, first_block, blocks, block_total):
    key_block = jnp.arange(block_total, dtype=jnp.int32)
    here = first_block + jnp.arange(blocks, dtype=jnp.int32)
    column = jnp.any(vertical[None] == key_block[:, None, None], axis=-1)
    gap = here[None, :] - key_block[:, None]
    diagonal = jnp.any(slash[None, :, None, :] == gap[:, None, :, None], axis=-1)
    allowed = column[:, :, None] | diagonal
    earlier = (key_block < first_block)[:, None, None]
    width = QUERY_HEADS * blocks

    def spread(keep):
        fill = jnp.where(keep, 0.0, MASKED).astype(jnp.bfloat16).reshape(-1, width)
        return jnp.repeat(fill, BLOCK, axis=0)

    own = lax.dynamic_slice_in_dim(allowed, first_block, blocks, 0)
    return spread(allowed & earlier), spread(own)


def body(queries, keys, values, vertical, slash):
    rows = queries.shape[0]
    ways = lax.axis_size("rep") * lax.axis_size("seq")
    tokens = rows * ways
    position = lax.axis_index("rep") * lax.axis_size("seq") + lax.axis_index("seq")
    total_bytes = 2 * tokens * keys.shape[1] * keys.dtype.itemsize
    tight = total_bytes > (32 << 20)
    heads = 1
    mask, own_mask = mask_columns(
        vertical, slash, position * (rows // BLOCK), rows // BLOCK, tokens // BLOCK
    )
    if not tight and lax.axis_size("rep") == 4 and lax.axis_size("seq") % 2 == 0:
        return fused(queries, keys, values, mask, own_mask, lax.axis_size("seq") // 2)
    position = position.astype(jnp.int32).reshape(1)
    out = None
    for first in range(0, KEY_VALUE_HEADS, heads):
        columns = slice(first * HEAD_SIZE, (first + heads) * HEAD_SIZE)
        part = jnp.concatenate([keys[:, columns], values[:, columns]], axis=1)
        if tight and out is not None:
            part, out = lax.optimization_barrier((part, out))
        gathered = lax.all_gather(part, ("rep", "seq"), axis=0, tiled=True)
        out = attend(position, queries, gathered, mask, own_mask, out, first, heads)
    return out


def solution(mesh):
    in_specs = (P(("rep", "seq"), None), P(("rep", "seq"), None), P(("rep", "seq"), None), P(), P())
    out_specs = P(("rep", "seq"), None)
    return jax.shard_map(body, mesh=mesh, in_specs=in_specs, out_specs=out_specs, check_vma=False)
```

```python
import functools
import math

import jax
import jax.numpy as jnp
from jax import lax
from jax.experimental import pallas as pl
from jax.experimental.pallas import tpu as pltpu
from jax.sharding import PartitionSpec as P

QUERY_HEADS = 64
KEY_VALUE_HEADS = 8
HEAD_SIZE = 128
BLOCK = 64
GROUP = QUERY_HEADS // KEY_VALUE_HEADS

MASKED = -1e30
KEY_TILE = 1024
ROW_TILE = 256
EXP2_SCALE = math.log2(math.e) / math.sqrt(HEAD_SIZE)


def attend_kernel(first_head, rows, position_ref, q_ref, k_ref, v_ref, mask_ref, own_mask_ref, *rest):
    out_ref, query_s, best_s, acc_s = rest[-4:]
    blocks = rows // BLOCK
    position = position_ref[0]
    head_base = (first_head + pl.program_id(0)) * GROUP
    lane = lax.broadcasted_iota(jnp.int32, (rows, HEAD_SIZE), 1)
    row_block = lax.broadcasted_iota(jnp.int32, (rows, HEAD_SIZE), 0) // BLOCK
    for head in range(GROUP):
        pick = lane == (head_base + head) * blocks + row_block
        query_s[head * rows : (head + 1) * rows, :HEAD_SIZE] = q_ref[
            :, head * HEAD_SIZE : (head + 1) * HEAD_SIZE
        ]
        query_s[head * rows : (head + 1) * rows, HEAD_SIZE:] = pick.astype(jnp.bfloat16)

    row_tile = min(ROW_TILE, GROUP * rows)
    tiles = [slice(i, i + row_tile) for i in range(0, GROUP * rows, row_tile)]
    contract = (((1,), (1,)), ((), ()))

    own = pl.ds(pl.multiple_of(position * rows, rows), rows)
    own_keys = jnp.concatenate([k_ref[own, :], own_mask_ref[...]], axis=1)
    own_values = jnp.concatenate([v_ref[own, :], jnp.ones((rows, HEAD_SIZE), jnp.bfloat16)], axis=1)
    own_row = lax.broadcasted_iota(jnp.int32, (row_tile, rows), 0) % rows
    own_column = lax.broadcasted_iota(jnp.int32, (row_tile, rows), 1)
    for tile in tiles:
        scores = lax.dot_general(
            query_s[tile, :], own_keys, contract, preferred_element_type=jnp.float32
        )
        scores = jnp.where(own_column <= own_row, scores, MASKED)
        best = jnp.max(scores, axis=1, keepdims=True)
        weights = jnp.exp2((scores - best) * EXP2_SCALE).astype(jnp.bfloat16)
        best_s[tile, :] = jnp.broadcast_to(best, (row_tile, HEAD_SIZE))
        acc_s[tile, :] = jnp.dot(weights, own_values, preferred_element_type=jnp.float32)

    def key_step(step, _):
        here = pl.ds(pl.multiple_of(step * KEY_TILE, KEY_TILE), KEY_TILE)
        keys = jnp.concatenate([k_ref[here, :], mask_ref[here, :]], axis=1)
        values = jnp.concatenate(
            [v_ref[here, :], jnp.ones((KEY_TILE, HEAD_SIZE), jnp.bfloat16)], axis=1
        )
        for tile in tiles:
            scores = lax.dot_general(
                query_s[tile, :], keys, contract, preferred_element_type=jnp.float32
            )
            before = best_s[tile, :1]
            best = jnp.maximum(before, jnp.max(scores, axis=1, keepdims=True))
            factor = jnp.exp2((before - best) * EXP2_SCALE)
            weights = jnp.exp2((scores - best) * EXP2_SCALE).astype(jnp.bfloat16)
            best_s[tile, :] = jnp.broadcast_to(best, (row_tile, HEAD_SIZE))
            acc_s[tile, :] = acc_s[tile, :] * factor + jnp.dot(
                weights, values, preferred_element_type=jnp.float32
            )
        return 0

    lax.fori_loop(0, (position * rows + KEY_TILE - 1) // KEY_TILE, key_step, 0)

    for head in range(GROUP):
        tile = slice(head * rows, (head + 1) * rows)
        out_ref[:, head * HEAD_SIZE : (head + 1) * HEAD_SIZE] = (
            acc_s[tile, :HEAD_SIZE] / acc_s[tile, HEAD_SIZE:]
        ).astype(jnp.bfloat16)


def attend(position, queries, gathered, mask, own_mask, out, first_head, heads):
    rows = queries.shape[0]
    tokens = gathered.shape[0]
    once = pl.Buffered(1)
    in_specs = [
        pl.BlockSpec((rows, GROUP * HEAD_SIZE), lambda g, s: (0, first_head + g)),
        pl.BlockSpec((tokens, HEAD_SIZE), lambda g, s: (0, g)),
        pl.BlockSpec((tokens, HEAD_SIZE), lambda g, s: (0, heads + g)),
        pl.BlockSpec((tokens, HEAD_SIZE), lambda g, s: (0, 0), pipeline_mode=once),
        pl.BlockSpec((rows, HEAD_SIZE), lambda g, s: (0, 0), pipeline_mode=once),
    ]
    operands = [position, queries, gathered, gathered, mask, own_mask]
    aliases = {}
    if out is not None:
        in_specs.append(pl.BlockSpec(memory_space=pl.ANY))
        aliases = {len(operands): 0}
        operands.append(out)
    pairs = heads * GROUP * rows * tokens
    return pl.pallas_call(
        functools.partial(attend_kernel, first_head, rows),
        out_shape=jax.ShapeDtypeStruct(queries.shape, jnp.bfloat16),
        grid_spec=pltpu.PrefetchScalarGridSpec(
            num_scalar_prefetch=1,
            grid=(heads,),
            in_specs=in_specs,
            out_specs=pl.BlockSpec((rows, GROUP * HEAD_SIZE), lambda g, s: (0, first_head + g)),
            scratch_shapes=[
                pltpu.VMEM((GROUP * rows, 2 * HEAD_SIZE), jnp.bfloat16),
                pltpu.VMEM((GROUP * rows, HEAD_SIZE), jnp.float32),
                pltpu.VMEM((GROUP * rows, 2 * HEAD_SIZE), jnp.float32),
            ],
        ),
        input_output_aliases=aliases,
        compiler_params=pltpu.CompilerParams(
            vmem_limit_bytes=60 << 20
        ),
        cost_estimate=pl.CostEstimate(
            flops=pairs * HEAD_SIZE * 8,
            bytes_accessed=heads * tokens * HEAD_SIZE * 4,
            transcendentals=pairs,
        ),
    )(*operands)


def fused_kernel(
    q_ref, key_ref, value_ref, column_ref, offset_ref, out_ref,
    pool, mask_ref, own_mask_ref, bias_s, query_s, best_s, acc_s, send_sem, recv_sem,
):
    rows = key_ref.shape[0]
    depth = pool.shape[4]
    blocks = rows // BLOCK
    seq, rep = lax.axis_index("seq"), lax.axis_index("rep")
    z, x, y, core = seq // 2, seq % 2, rep // 2, rep % 2
    z_peers = [((z + k) % depth) * 2 + x for k in range(1, depth)]
    along_x = {"seq": z * 2 + 1 - x, "rep": rep}
    along_y = {"seq": seq, "rep": (1 - y) * 2 + core}
    sibling = {"seq": seq, "rep": y * 2 + 1 - core}
    peers = [{"seq": peer, "rep": rep} for peer in z_peers] + [along_x, along_y, sibling]

    for head in range(KEY_VALUE_HEADS):
        columns = slice(head * HEAD_SIZE, (head + 1) * HEAD_SIZE)
        pool[0, head, y, core, z, x] = key_ref[:, columns]
        pool[1, head, y, core, z, x] = value_ref[:, columns]

    barrier = pltpu.get_barrier_semaphore()
    for peer in peers:
        pl.semaphore_signal(
            barrier, inc=1, device_id=peer, device_id_type=pl.DeviceIdType.MESH
        )
    pl.semaphore_wait(barrier, len(peers))

    copies = {}

    def send(kind, part, slot, ref, peer):
        copy = pltpu.make_async_remote_copy(
            src_ref=ref,
            dst_ref=ref,
            send_sem=send_sem.at[kind, part, slot],
            recv_sem=recv_sem.at[kind, part, slot],
            device_id=peer,
            device_id_type=pl.DeviceIdType.MESH,
        )
        copy.start()
        copies[kind, part, slot] = copy

    def heads_of(part):
        return part

    def stage_line(part):
        for kind in range(2):
            for k in range(depth - 1):
                send(kind, part, k, pool.at[kind, heads_of(part), y, core, z, x], peers[k])

    def stage_first(part):
        for kind in range(2):
            for k in range(depth - 1):
                copies[kind, part, k].wait_recv()
            send(
                kind, part, depth - 1, pool.at[kind, heads_of(part), y, core, :, x],
                along_y if kind else along_x,
            )

    def stage_second(part):
        for kind in range(2):
            copies[kind, part, depth - 1].wait_recv()
        send(0, part, depth, pool.at[0, heads_of(part), y, core], along_y)
        send(1, part, depth, pool.at[1, heads_of(part), :, core, :, x], along_x)

    def stage_core(part):
        for kind in range(2):
            copies[kind, part, depth].wait_recv()
            send(kind, part, depth + 1, pool.at[kind, heads_of(part), :, core], sibling)

    def stage_done(part):
        for kind in range(2):
            copies[kind, part, depth + 1].wait_recv()

    key_tile = depth * 2 * rows
    steps = rep + (seq + 2 * depth - 1) // (2 * depth)
    contract = (((1,), (1,)), ((), ()))

    first_block = (rep * (2 * depth) + seq) * blocks

    def allowed_blocks(key_block):
        gap = first_block + lax.broadcasted_iota(jnp.int32, key_block.shape, 1) % blocks - key_block
        allowed = (column_ref[:1, :] == key_block) | (offset_ref[:1, :] == gap)
        for slot in range(1, column_ref.shape[0]):
            allowed = allowed | (column_ref[slot : slot + 1, :] == key_block)
        for slot in range(1, offset_ref.shape[0]):
            allowed = allowed | (offset_ref[slot : slot + 1, :] == gap)
        return allowed

    def build_masks():
        key_block = lax.broadcasted_iota(jnp.int32, bias_s.shape, 0)
        keep = allowed_blocks(key_block) & (key_block < first_block)
        bias_s[...] = jnp.where(keep, 0.0, MASKED)
        for block in range(bias_s.shape[0]):
            mask_ref[block * BLOCK : (block + 1) * BLOCK, :] = jnp.broadcast_to(
                bias_s[block : block + 1, :], (BLOCK, HEAD_SIZE)
            ).astype(jnp.bfloat16)
        own_block = first_block + (
            lax.broadcasted_iota(jnp.int32, own_mask_ref.shape, 0) // BLOCK
        )
        own_mask_ref[...] = jnp.where(allowed_blocks(own_block), 0.0, MASKED).astype(jnp.bfloat16)

    def attend_heads(group, locals_here):
        lane = lax.broadcasted_iota(jnp.int32, (rows, HEAD_SIZE), 1)
        row_block = lax.broadcasted_iota(jnp.int32, (rows, HEAD_SIZE), 0) // BLOCK
        for place, local in enumerate(locals_here):
            head = group * GROUP + local
            here = slice(place * rows, (place + 1) * rows)
            query_s[here, :HEAD_SIZE] = q_ref[:, head * HEAD_SIZE : (head + 1) * HEAD_SIZE]
            query_s[here, HEAD_SIZE:] = (lane == head * blocks + row_block).astype(jnp.bfloat16)

        row_tile = min(ROW_TILE, len(locals_here) * rows)
        tiles = [slice(i, i + row_tile) for i in range(0, len(locals_here) * rows, row_tile)]

        def logits(keys):
            return [
                lax.dot_general(
                    query_s[tile, :], keys, contract, preferred_element_type=jnp.float32
                )
                for tile in tiles
            ]

        own_keys = jnp.concatenate([pool[0, group, y, core, z, x], own_mask_ref[...]], axis=1)
        own_values = jnp.concatenate(
            [pool[1, group, y, core, z, x], jnp.ones((rows, HEAD_SIZE), jnp.bfloat16)], axis=1
        )
        own_row = lax.broadcasted_iota(jnp.int32, (row_tile, rows), 0) % rows
        own_column = lax.broadcasted_iota(jnp.int32, (row_tile, rows), 1)
        for tile, scores in zip(tiles, logits(own_keys)):
            scores = jnp.where(own_column <= own_row, scores, MASKED)
            best = jnp.max(scores, axis=1, keepdims=True)
            weights = jnp.exp2((scores - best) * EXP2_SCALE).astype(jnp.bfloat16)
            best_s[tile, :] = jnp.broadcast_to(best, (row_tile, HEAD_SIZE))
            acc_s[tile, :] = jnp.dot(weights, own_values, preferred_element_type=jnp.float32)

        def key_step(step, _):
            here = pl.ds(pl.multiple_of(step * key_tile, key_tile), key_tile)
            key_rows = pool[0, group, step // 2, step % 2].reshape(key_tile, HEAD_SIZE)
            value_rows = pool[1, group, step // 2, step % 2].reshape(key_tile, HEAD_SIZE)
            keys = jnp.concatenate([key_rows, mask_ref[here, :]], axis=1)
            values = jnp.concatenate(
                [value_rows, jnp.ones((key_tile, HEAD_SIZE), jnp.bfloat16)], axis=1
            )
            for tile, scores in zip(tiles, logits(keys)):
                before = best_s[tile, :1]
                best = jnp.maximum(before, jnp.max(scores, axis=1, keepdims=True))
                factor = jnp.exp2((before - best) * EXP2_SCALE)
                weights = jnp.exp2((scores - best) * EXP2_SCALE).astype(jnp.bfloat16)
                best_s[tile, :] = jnp.broadcast_to(best, (row_tile, HEAD_SIZE))
                acc_s[tile, :] = acc_s[tile, :] * factor + jnp.dot(
                    weights, values, preferred_element_type=jnp.float32
                )
            return 0

        lax.fori_loop(0, steps, key_step, 0)
        for place, local in enumerate(locals_here):
            head = group * GROUP + local
            tile = slice(place * rows, (place + 1) * rows)
            out_ref[:, head * HEAD_SIZE : (head + 1) * HEAD_SIZE] = (
                acc_s[tile, :HEAD_SIZE] / acc_s[tile, HEAD_SIZE:]
            ).astype(jnp.bfloat16)

    parts = KEY_VALUE_HEADS
    for part in range(parts):
        stage_line(part)
    build_masks()

    def run(stage, part):
        if part < parts:
            stage(part)

    stage_first(0)
    stage_second(0)
    stage_first(1)
    stage_core(0)
    stage_second(1)
    stage_first(2)
    stage_done(0)
    for part in range(parts):
        attend_heads(part, range(GROUP // 2))
        run(stage_core, part + 1)
        run(stage_second, part + 2)
        attend_heads(part, range(GROUP // 2, GROUP))
        run(stage_first, part + 3)
        run(stage_done, part + 1)
    for copy in copies.values():
        copy.wait_send()


def fused(queries, keys, values, vertical, slash, depth):
    rows = queries.shape[0]
    parts = KEY_VALUE_HEADS
    tokens = rows * 8 * depth
    blocks = rows // BLOCK
    tables = [jnp.repeat(table.T, blocks, axis=1) for table in (vertical, slash)]
    half = GROUP * rows // 2
    pairs = QUERY_HEADS * rows * tokens
    whole = pl.BlockSpec(memory_space=pltpu.VMEM)
    return pl.pallas_call(
        fused_kernel,
        out_shape=jax.ShapeDtypeStruct(queries.shape, jnp.bfloat16),
        in_specs=[whole] * 5,
        out_specs=whole,
        scratch_shapes=[
            pltpu.VMEM((2, KEY_VALUE_HEADS, 2, 2, depth, 2, rows, HEAD_SIZE), jnp.bfloat16),
            pltpu.VMEM((tokens, HEAD_SIZE), jnp.bfloat16),
            pltpu.VMEM((rows, HEAD_SIZE), jnp.bfloat16),
            pltpu.VMEM((tokens // BLOCK, HEAD_SIZE), jnp.float32),
            pltpu.VMEM((half, 2 * HEAD_SIZE), jnp.bfloat16),
            pltpu.VMEM((half, HEAD_SIZE), jnp.float32),
            pltpu.VMEM((half, 2 * HEAD_SIZE), jnp.float32),
            pltpu.SemaphoreType.DMA((2, parts, depth + 2)),
            pltpu.SemaphoreType.DMA((2, parts, depth + 2)),
        ],
        compiler_params=pltpu.CompilerParams(
            collective_id=0, has_side_effects=True, vmem_limit_bytes=56 << 20
        ),
        cost_estimate=pl.CostEstimate(
            flops=pairs * HEAD_SIZE * 8, bytes_accessed=8 << 20, transcendentals=pairs
        ),
    )(queries, keys, values, *tables)


def mask_columns(vertical, slash, first_block, blocks, block_total):
    key_block = jnp.arange(block_total, dtype=jnp.int32)
    here = first_block + jnp.arange(blocks, dtype=jnp.int32)
    column = jnp.any(vertical[None] == key_block[:, None, None], axis=-1)
    gap = here[None, :] - key_block[:, None]
    diagonal = jnp.any(slash[None, :, None, :] == gap[:, None, :, None], axis=-1)
    allowed = column[:, :, None] | diagonal
    earlier = (key_block < first_block)[:, None, None]
    width = QUERY_HEADS * blocks

    def spread(keep):
        fill = jnp.where(keep, 0.0, MASKED).astype(jnp.bfloat16).reshape(-1, width)
        return jnp.repeat(fill, BLOCK, axis=0)

    own = lax.dynamic_slice_in_dim(allowed, first_block, blocks, 0)
    return spread(allowed & earlier), spread(own)


def body(queries, keys, values, vertical, slash):
    rows = queries.shape[0]
    ways = lax.axis_size("rep") * lax.axis_size("seq")
    tokens = rows * ways
    position = lax.axis_index("rep") * lax.axis_size("seq") + lax.axis_index("seq")
    total_bytes = 2 * tokens * keys.shape[1] * keys.dtype.itemsize
    tight = total_bytes > (32 << 20)
    heads = 1
    staged = rows == 2 * BLOCK and lax.axis_size("rep") == 4 and lax.axis_size("seq") % 2 == 0
    if staged and not tight:
        return fused(queries, keys, values, vertical, slash, lax.axis_size("seq") // 2)
    mask, own_mask = mask_columns(
        vertical, slash, position * (rows // BLOCK), rows // BLOCK, tokens // BLOCK
    )
    position = position.astype(jnp.int32).reshape(1)
    out = None
    for first in range(0, KEY_VALUE_HEADS, heads):
        columns = slice(first * HEAD_SIZE, (first + heads) * HEAD_SIZE)
        part = jnp.concatenate([keys[:, columns], values[:, columns]], axis=1)
        if tight and out is not None:
            part, out = lax.optimization_barrier((part, out))
        gathered = lax.all_gather(part, ("rep", "seq"), axis=0, tiled=True)
        out = attend(position, queries, gathered, mask, own_mask, out, first, heads)
    return out


def solution(mesh):
    in_specs = (P(("rep", "seq"), None), P(("rep", "seq"), None), P(("rep", "seq"), None), P(), P())
    out_specs = P(("rep", "seq"), None)
    return jax.shard_map(body, mesh=mesh, in_specs=in_specs, out_specs=out_specs, check_vma=False)
```
